32 devices in a mesh: pair: 16 (over z, y, x), aux: 2 (over core).
Axes of the slice: x: 2, y: 2, z: 4, core: 2. Of those that a mesh axis runs over, the one named last changes fastest.
Arguments:
- amplitudes: bfloat16 [2048, 128, 128], P('pair', 'aux'), may hold values from -6 to 6
- k_term: bfloat16 [2048, 128, 128], P('pair', 'aux'), may hold values from -6 to 6
- margin_table: bfloat16 [128, 128, 128], P('pair'), may hold values from -0.5 to 0.5
- margin_index: int32 [2048], P('pair'), may hold values from 0 to 7
- factors: bfloat16 [16, 512, 128], P('pair', 'aux'), may hold values from -6 to 6
- vir_energy: float32 [2048, 128], P('pair'), may hold values from 0.5 to 3
- occ_energy: float32 [16], replicated, may hold values from -2 to -0.3
- pair_owner: int32 [2048, 1], P('pair'), may hold values from 0 to 15; in each aligned block of 128 rows (0 to 127, 128 to 255, ...) at most 16 rows name the same one
Outputs:
- updated: bfloat16 [2048, 128, 128], P('pair', 'aux')
The draws below stay inside these ranges and needn't reach their ends.
Inputs may be any that keep to these rules, and one draw needn't show every extreme that they name: `pair_owner`: no more than 16 of the 128 pairs of one aligned block name the same owner. `margin_index`: an index into the 8 margin blocks that belong to the pair's aligned block of 128 pairs.
All inputs are finite; a program needn't handle non-finite values.
Results may differ from the reference program's by a relative error of at most 0.0055.
Values may be sent and summed in bfloat16 or wider, within the bound.
A program may use at most 128 MiB of HBM per device.

```python
import math
import jax
import jax.numpy as jnp
import numpy as np
from jax import lax

NV = 128
NAUX = 512
OVL_DEV = 8
PAIR_DEV = 128
CAP = 16
NOCC = 16
NPAIRS = 2048
N_PAIR = 16


def plant(array, stream_key, low, largest):
    dims = array.shape
    index_at = [jax.random.randint(jax.random.fold_in(stream_key, axis), (), 0, dims[axis]) for axis in range(len(dims))]
    array = array.at[tuple(index_at)].set(low)
    longest = dims.index(max(dims))
    index_at[longest] = (index_at[longest] + 1) % dims[longest]
    return array.at[tuple(index_at)].set(largest)


def block_scale(own_key, dims, cuts, smallest, high):
    level = 1.0
    for axis_at, parts in cuts:
        heights = jax.random.uniform(jax.random.fold_in(jax.random.fold_in(own_key, 6), axis_at), (parts,), jnp.float32, smallest / len(cuts), high / len(cuts))
        level = level * jnp.repeat(jnp.exp(heights), dims[axis_at] // parts).reshape((-1,) + (1,) * (len(dims) - 1 - axis_at))
    return level


def deal_out(own_key, own, number, rows, count, top, most, lean):
    ranking = jax.random.permutation(own_key, count)
    crowded, common = shares(count, rows * top, most, lean, True), shares(count, rows * top, most, lean, False)
    places = jnp.arange(count)

    def named(lengths, rotation):
        used = int((lengths > 0).sum())
        fixed = max(1, used // 4)
        moved = fixed + (places - fixed + rotation * (used - fixed)) % max(1, count - fixed)
        return jnp.zeros((count,), jnp.int32).at[ranking[jnp.where(places < fixed, places, moved)]].set(jnp.asarray(lengths, jnp.int32))

    lengths = jnp.where(number % 4 == 0, named(crowded, number // 4), named(common, number - number // 4 - 1))
    mixed = jax.random.permutation(jax.random.fold_in(own, 3), count)
    giver, taker = mixed[0:count // 2 * 2:2], mixed[1:count // 2 * 2:2]
    room = jnp.minimum(lengths[giver] - 1, most - lengths[taker]) // 2
    room = jnp.where((giver == ranking[0]) | (taker == ranking[0]) | (lengths[taker] == 0), 0, jnp.maximum(room, 0))
    moved = jax.random.randint(jax.random.fold_in(own, 4), (count // 2,), 0, 1 << 20) % (room + 1)
    lengths = lengths.at[giver].add(-moved).at[taker].add(moved)
    items = jnp.searchsorted(jnp.cumsum(lengths), jnp.arange(rows * top), side="right").astype(jnp.int32)
    table = items.reshape(top, rows).T
    table = table[jax.random.permutation(jax.random.fold_in(own, 1), rows)]
    rotation = jax.random.randint(jax.random.fold_in(own, 2), (rows, 1), 0, top)
    return jnp.take_along_axis(table, (jnp.arange(top)[None, :] + rotation) % top, axis=1)


def shares(count, total, limit, lean, full):
    portions = [(1 << 20) // math.isqrt(grade ** lean) + 1 for grade in range(1, count + 1)]
    largest = limit if full else min(limit, max(-(-total // count), total * portions[0] // sum(portions)))
    least = 1 if total - largest >= count - 1 else 0
    holding, rest = [largest] + [least] * (count - 1), total - largest - least * (count - 1)
    while rest > 0:
        movable = [i for i in range(1, count) if holding[i] < largest] or [i for i in range(1, count) if holding[i] < limit]
        whole, remaining = sum([portions[i] for i in movable]), rest
        for i in movable:
            extra = min(limit - holding[i], max(1, remaining * portions[i] // whole), rest)
            holding[i] = holding[i] + extra
            rest = rest - extra
    return np.array(holding)


def bell_draw(key, dims, spread, reach, pieces=(), held_as=jnp.bfloat16):
    loudness = block_scale(key, dims, pieces, -0.22, 0.18) if pieces else 1.0
    array = jax.random.normal(key, dims, jnp.float32) * spread * loudness
    return jnp.minimum(jnp.maximum(array, -reach), reach).astype(held_as)


def setup_inputs(seed: int = 0) -> dict:
    seeds = jax.random.split(jax.random.key(seed), 9)
    amplitudes = bell_draw(seeds[0], (NPAIRS, NV, NV), 1.0, 6.0, ((0, 16), (1, 2)))
    k_term = bell_draw(seeds[1], (NPAIRS, NV, NV), 1.0, 6.0, ((0, 16), (1, 2)))
    margin_table = bell_draw(seeds[2], (N_PAIR * OVL_DEV, NV, NV), NV ** -0.5, 0.5, ((0, 16),))
    margin_index = plant(jax.random.randint(seeds[3], (NPAIRS,), 0, OVL_DEV), jax.random.fold_in(seeds[3], 1), 0, OVL_DEV - 1).astype(jnp.int32)
    factors = bell_draw(seeds[4], (NOCC, NAUX, NV), 1.0, 6.0, ((0, 16), (1, 2)))
    vir_energy = jnp.clip(0.5 + 2.5 * jax.random.uniform(seeds[5], (NPAIRS, NV), jnp.float32) ** block_scale(seeds[5], (NPAIRS, NV), ((0, 16),), -0.2, 0.2), 0.5, 3.0)
    occ_energy = jnp.clip(jax.random.uniform(seeds[6], (NOCC,), jnp.float32, -2.0, -0.3), -2.0, -0.3)
    pair_owner_keys = jax.random.split(jax.random.fold_in(seeds[7], 1), NPAIRS // PAIR_DEV)
    pair_owner_turns = jax.random.permutation(jax.random.fold_in(seeds[7], 3), NPAIRS // PAIR_DEV)
    pair_owner = jax.vmap(lambda own, number: deal_out(jax.random.fold_in(seeds[7], 2), own, number, PAIR_DEV, N_PAIR, 1, CAP, 2))(pair_owner_keys, pair_owner_turns).reshape((NPAIRS, 1))
    return dict(amplitudes=amplitudes, k_term=k_term, margin_table=margin_table, margin_index=margin_index, factors=factors, vir_energy=vir_energy, occ_energy=occ_energy, pair_owner=pair_owner)


def rounded(values):
    return lax.optimization_barrier(values.astype(jnp.bfloat16)).astype(jnp.float32)


def reference(amplitudes, k_term, margin_table, margin_index, factors, vir_energy, occ_energy, pair_owner):
    position = jnp.arange(N_PAIR * PAIR_DEV, dtype=jnp.int32)
    block_index = (position // PAIR_DEV).astype(jnp.int32)
    occ_first = block_index
    occ_second = pair_owner[:, 0].astype(jnp.int32)
    margin_row = (block_index * OVL_DEV + margin_index).astype(jnp.int32)
    cycle_scale = float(NV * NAUX * PAIR_DEV) ** -0.5

    def blocks(values):
        return values.reshape((N_PAIR, PAIR_DEV) + values.shape[1:])

    def dress(dressed, inputs):
        amp_block, rows_ovl, first, second = inputs
        margin = margin_table[rows_ovl].astype(jnp.float32)
        halfway = rounded(jnp.einsum('pca,pab->pcb', amp_block.astype(jnp.float32), margin))
        rotated = rounded(jnp.einsum('pac,pab->pcb', margin, halfway))
        factor_rows = factors[first].astype(jnp.float32)
        partial_value = rounded(jnp.einsum('pca,pqa->pcq', rotated, factor_rows))
        return dressed.at[second].add(partial_value), None

    start = jnp.zeros((N_PAIR, NV, NAUX), jnp.float32)
    dressed, _ = lax.scan(dress, start, (blocks(amplitudes), blocks(margin_row), blocks(occ_first), blocks(occ_second)))
    cycle_table = rounded(cycle_scale * jnp.einsum('jcq,jqa->jca', rounded(dressed), factors.astype(jnp.float32)))

    def update(inputs):
        amp_block, k_block, rows_ovl, first, second, energy = inputs
        margin = margin_table[rows_ovl].astype(jnp.float32)
        own_cycle = cycle_table[second]
        cycle_term = jnp.einsum('pca,pba->pcb', own_cycle, margin)
        occ_sum = occ_energy[first] + occ_energy[second]
        denominator = energy[:, :, None] + energy[:, None, :] - occ_sum[:, None, None]
        return (amp_block.astype(jnp.float32) - (cycle_term + k_block.astype(jnp.float32)) / denominator).astype(jnp.bfloat16)

    result = lax.map(update, (blocks(amplitudes), blocks(k_term), blocks(margin_row), blocks(occ_first), blocks(occ_second), blocks(vir_energy)))
    return result.reshape(amplitudes.shape)
```

```python
import functools

import jax
import jax.numpy as jnp
from jax import lax
from jax.experimental import pallas as pl
from jax.experimental.pallas import tpu as pltpu
from jax.sharding import PartitionSpec as P

MESH = pl.DeviceIdType.MESH
VMEM_BYTES = 56 * 1024 * 1024
GROUP = 16
CHUNKS = 4


def dot(a, b):
    return jnp.dot(a, b, preferred_element_type=jnp.float32)


def cycle_kernel(
    sizes, scale,
    last_ref, amp_hbm, fac_hbm, table_ref, cyc_out,
    amp, prefix, stacked, half, margin_t, r_send, r_own, r_recv, r_sum, r_in,
    f_plane, f_col, g_own, g_send, g_recv, g_sum, c_own, c_send, c_recv, cyc,
    amp_sem, loc_sem, fp_s, fp_r, fz_s, fz_r, sib_s, sib_r, r_s, r_r, c_s, c_r, az_s, ap_s, ag_r,
):
    count, planes, cols, tables = sizes
    rows = amp.shape[1]
    pairs = amp.shape[0]
    me, h = lax.axis_index("pair"), lax.axis_index("aux")
    col, plane = lax.div(me, planes), lax.rem(me, planes)
    sibling = (me, 1 - h)
    plane_peers = [lax.rem(plane + d, planes) for d in range(1, planes)]
    col_peers = [lax.rem(col + d, cols) for d in range(1, cols)]

    def at_plane(t):
        return (col * planes + t, h)

    def at_col(z):
        return (z * planes + plane, h)

    def remote(src, dst, send, recv, device):
        return pltpu.make_async_remote_copy(
            src_ref=src, dst_ref=dst, send_sem=send, recv_sem=recv,
            device_id=device, device_id_type=MESH,
        )

    step = pairs // CHUNKS
    loads = []
    for k in range(CHUNKS):
        part = pl.ds(k * step, step)
        loads.append(pltpu.make_async_copy(amp_hbm.at[part], amp.at[part], amp_sem.at[k]))
        loads[-1].start()
    own_plane = pltpu.make_async_copy(fac_hbm.at[0], f_plane.at[plane], loc_sem.at[0])
    own_col = pltpu.make_async_copy(fac_hbm.at[0], f_col.at[col], loc_sem.at[1])
    own_plane.start()
    own_col.start()

    barrier = pltpu.get_barrier_semaphore()
    for device in [sibling] + [at_plane(t) for t in plane_peers] + [at_col(z) for z in col_peers]:
        pl.semaphore_signal(barrier, inc=1, device_id=device, device_id_type=MESH)
    pl.semaphore_wait(barrier, 1 + (planes - 1) + (cols - 1))

    sends = []
    for z in col_peers:
        sends.append(remote(fac_hbm.at[0], f_col.at[col], fz_s.at[z], fz_r.at[col], at_col(z)))
        sends[-1].start()
    for t in plane_peers:
        sends.append(remote(fac_hbm.at[0], f_plane.at[plane], fp_s.at[t], fp_r.at[plane], at_plane(t)))
        sends[-1].start()

    prefix[pairs] = jnp.zeros(prefix.shape[1:], jnp.float32)
    for m in range(tables):
        piece = table_ref[m, pl.ds(pl.multiple_of(h * rows, rows), rows), :]
        margin_t[:, m * rows : (m + 1) * rows] = piece.T

    for k in range(CHUNKS):
        loads[k].wait()

        def add_pair(p, carry):
            prefix[p] = amp[p].astype(jnp.float32) + prefix[last_ref[p]]
            return carry

        lax.fori_loop(k * step, (k + 1) * step, add_pair, 0, unroll=4)

    other = margin_t[pl.ds(pl.multiple_of((1 - h) * rows, rows), rows), :]
    mine = margin_t[pl.ds(pl.multiple_of(h * rows, rows), rows), :]

    def rotate(g, carry):
        base = g * GROUP
        for m in range(tables):
            for o in range(GROUP):
                found = last_ref[pairs + (base + o) * tables + m]
                stacked[m, o * rows : (o + 1) * rows, :] = prefix[found].astype(jnp.bfloat16)
        for m in range(tables):
            for o in range(0, GROUP, 4):
                value = dot(stacked[m, o * rows : (o + 4) * rows, :], table_ref[m]).astype(jnp.bfloat16)
                for u in range(4):
                    half[m * rows : (m + 1) * rows, (o + u) * 128 : (o + u + 1) * 128] = value[
                        u * rows : (u + 1) * rows
                    ]
        for o in range(0, GROUP, 2):
            value = dot(other, half[:, o * 128 : (o + 2) * 128])
            for u in range(2):
                r_send[base + o + u] = value[:, u * 128 : (u + 1) * 128].astype(jnp.bfloat16)
        for o in range(0, GROUP, 2):
            value = dot(mine, half[:, o * 128 : (o + 2) * 128])
            for u in range(2):
                r_own[base + o + u] = value[:, u * 128 : (u + 1) * 128]
        return carry

    lax.fori_loop(0, count // GROUP, rotate, 0)

    swap_r = remote(r_send, r_recv, sib_s.at[0], sib_r.at[0], sibling)
    swap_r.start()

    own_plane.wait()
    own_col.wait()
    for t in plane_peers:
        remote(fac_hbm.at[0], f_plane.at[t], fp_s.at[t], fp_r.at[t], at_plane(t)).wait_recv()
    for z in col_peers:
        remote(fac_hbm.at[0], f_col.at[z], fz_s.at[z], fz_r.at[z], at_col(z)).wait_recv()

    def metric(z, carry):
        for s in range(planes):
            value = dot(f_plane[s].T, f_col[z])
            g_own[z, s * 128 : (s + 1) * 128, :] = value
            g_send[z, s * 128 : (s + 1) * 128, :] = value.astype(jnp.bfloat16)
        return carry

    lax.fori_loop(0, cols, metric, 0)
    swap_g = remote(g_send, g_recv, sib_s.at[1], sib_r.at[1], sibling)
    swap_g.start()

    swap_r.wait()
    r_sum[...] = (r_own[...] + r_recv[...].astype(jnp.float32)).astype(jnp.bfloat16)
    for t in plane_peers:
        sends.append(
            remote(
                r_sum.at[pl.ds(t * cols, cols)], r_in.at[plane], r_s.at[t], r_r.at[plane], at_plane(t)
            )
        )
        sends[-1].start()
    r_in[plane] = r_sum[pl.ds(plane * cols, cols)]
    swap_g.wait()
    g_sum[...] = (g_own[...] + g_recv[...].astype(jnp.float32)).astype(jnp.bfloat16)
    for t in plane_peers:
        remote(
            r_sum.at[pl.ds(t * cols, cols)], r_in.at[t], r_s.at[t], r_r.at[t], at_plane(t)
        ).wait_recv()

    def contract(z, carry):
        left = jnp.concatenate([r_in[s, z] for s in range(planes)], axis=1)
        value = dot(left, g_sum[z])
        c_own[z] = value
        c_send[z] = value.astype(jnp.bfloat16)
        return carry

    lax.fori_loop(0, cols, contract, 0)
    for z in col_peers:
        sends.append(remote(c_send.at[z], c_recv.at[col], c_s.at[z], c_r.at[col], at_col(z)))
        sends[-1].start()
    total = c_own[col]
    for z in col_peers:
        remote(c_send.at[z], c_recv.at[z], c_s.at[z], c_r.at[z], at_col(z)).wait_recv()
        total = total + c_recv[z].astype(jnp.float32)
    cyc[col, plane] = (scale * total).astype(jnp.bfloat16)

    mine_cyc = cyc.at[col, plane]
    for z in col_peers:
        sends.append(remote(mine_cyc, mine_cyc, az_s.at[z], ag_r.at[col, plane], at_col(z)))
        sends[-1].start()
    for t in plane_peers:
        sends.append(remote(mine_cyc, mine_cyc, ap_s.at[col, t], ag_r.at[col, plane], at_plane(t)))
        sends[-1].start()
    for z in col_peers:
        block = cyc.at[z, plane]
        remote(block, block, az_s.at[z], ag_r.at[z, plane], at_col(z)).wait_recv()
        for t in plane_peers:
            sends.append(remote(block, block, ap_s.at[z, t], ag_r.at[z, plane], at_plane(t)))
            sends[-1].start()
    for t in plane_peers:
        for z in [col] + col_peers:
            block = cyc.at[z, t]
            remote(block, block, ap_s.at[z, t], ag_r.at[z, t], at_plane(t)).wait_recv()
    cyc_out[...] = cyc[...]
    for copy in sends:
        copy.wait_send()


def update_kernel(
    margin_ref, owner_ref, occ_ref, cyc_ref, table_ref, energy_all, energy_ref, amp_ref, k_ref,
    out_ref, term, energy_t,
):
    tables, count = term.shape[0], term.shape[1]
    block, rows = amp_ref.shape[0], amp_ref.shape[1]
    step = pl.program_id(0)
    pairs = energy_all.shape[0]
    first = occ_ref[lax.axis_index("pair")]
    h = lax.axis_index("aux")

    @pl.when(step == 0)
    def _():
        energy_t[...] = energy_all[...].T

        def form(g, carry):
            at = pl.multiple_of(g * 4, 4)
            left = cyc_ref[pl.ds(at, 4)].reshape(4 * rows, 128)
            for m in range(tables):
                value = lax.dot_general(
                    left, table_ref[m], (((1,), (1,)), ((), ())), preferred_element_type=jnp.float32
                )
                term[m, pl.ds(at, 4)] = value.reshape(4, rows, 128)
            return carry

        lax.fori_loop(0, count // 4, form, 0)

    mine = energy_t[pl.ds(pl.multiple_of(h * rows, rows), rows), :]
    mine = pltpu.roll(mine, lax.rem(pairs - step * block, pairs), 1)
    for u in range(block):
        p = step * block + u
        owner = owner_ref[p]
        shift = first + occ_ref[owner]
        across = energy_ref[u : u + 1, :] - shift
        denominator = mine[:, u : u + 1] + across
        inverse = pl.reciprocal(denominator, approx=True)
        inverse = inverse * (2.0 - denominator * inverse)
        numerator = term[margin_ref[p], owner] + k_ref[u].astype(jnp.float32)
        out_ref[u] = (amp_ref[u].astype(jnp.float32) - numerator * inverse).astype(jnp.bfloat16)


def local(
    amplitudes, k_term, margin_table, margin_index, factors, vir_energy, occ_energy, pair_owner
):
    count = lax.axis_size("pair")
    aux_count = lax.axis_size("aux")
    pairs, rows, width = amplitudes.shape
    aux_rows = factors.shape[1]
    tables = margin_table.shape[0]
    planes = 4
    cols = count // planes
    scale = float(width * aux_rows * aux_count * pairs) ** (-0.5)
    bf16, f32 = jnp.bfloat16, jnp.float32

    owner = pair_owner[:, 0]
    slot = (owner % planes) * cols + owner // planes
    key = slot * tables + margin_index
    place = jnp.arange(pairs, dtype=jnp.int32)
    sought = jnp.concatenate([key, jnp.arange(count * tables, dtype=jnp.int32)])
    bound = jnp.concatenate([place, jnp.full((count * tables,), pairs, jnp.int32)])
    hit = (key[None, :] == sought[:, None]) & (place[None, :] < bound[:, None])
    last = jnp.max(jnp.where(hit, place[None, :], -1), axis=1)
    last = jnp.where(last < 0, pairs, last)

    dma = pltpu.SemaphoreType.DMA
    vmem = pl.BlockSpec(memory_space=pltpu.VMEM)
    smem = pl.BlockSpec(memory_space=pltpu.SMEM)
    anywhere = pl.BlockSpec(memory_space=pl.ANY)
    cyc = pl.pallas_call(
        functools.partial(cycle_kernel, (count, planes, cols, tables), scale),
        out_shape=jax.ShapeDtypeStruct((cols, planes, rows, width), bf16),
        in_specs=[smem, anywhere, anywhere, vmem],
        out_specs=vmem,
        scratch_shapes=[
            pltpu.VMEM((pairs, rows, width), bf16),
            pltpu.VMEM((pairs + 1, rows, width), f32),
            pltpu.VMEM((tables, GROUP * rows, width), bf16),
            pltpu.VMEM((tables * rows, GROUP * width), bf16),
            pltpu.VMEM((width, tables * rows), bf16),
            pltpu.VMEM((count, rows, width), bf16),
            pltpu.VMEM((count, rows, width), f32),
            pltpu.VMEM((count, rows, width), bf16),
            pltpu.VMEM((count, rows, width), bf16),
            pltpu.VMEM((planes, cols, rows, width), bf16),
            pltpu.VMEM((planes, aux_rows, width), bf16),
            pltpu.VMEM((cols, aux_rows, width), bf16),
            pltpu.VMEM((cols, planes * width, width), f32),
            pltpu.VMEM((cols, planes * width, width), bf16),
            pltpu.VMEM((cols, planes * width, width), bf16),
            pltpu.VMEM((cols, planes * width, width), bf16),
            pltpu.VMEM((cols, rows, width), f32),
            pltpu.VMEM((cols, rows, width), bf16),
            pltpu.VMEM((cols, rows, width), bf16),
            pltpu.VMEM((cols, planes, rows, width), bf16),
            dma((CHUNKS,)),
            dma((2,)),
            dma((planes,)),
            dma((planes,)),
            dma((cols,)),
            dma((cols,)),
            dma((2,)),
            dma((2,)),
            dma((planes,)),
            dma((planes,)),
            dma((cols,)),
            dma((cols,)),
            dma((cols,)),
            dma((cols, planes)),
            dma((cols, planes)),
        ],
        compiler_params=pltpu.CompilerParams(
            collective_id=0, has_side_effects=True, vmem_limit_bytes=VMEM_BYTES
        ),
        name="cycle",
    )(last, amplitudes, factors, margin_table)

    block = 16
    piece = pl.BlockSpec((block, rows, width), lambda s: (s, 0, 0))
    return pl.pallas_call(
        update_kernel,
        grid=(pairs // block,),
        out_shape=jax.ShapeDtypeStruct(amplitudes.shape, bf16),
        in_specs=[
            smem,
            smem,
            smem,
            vmem,
            vmem,
            vmem,
            pl.BlockSpec((block, width), lambda s: (s, 0)),
            piece,
            piece,
        ],
        out_specs=piece,
        scratch_shapes=[
            pltpu.VMEM((tables, count, rows, width), f32),
            pltpu.VMEM((width, pairs), f32),
        ],
        compiler_params=pltpu.CompilerParams(vmem_limit_bytes=VMEM_BYTES),
        name="update",
    )(
        margin_index, owner, occ_energy, cyc.reshape(count, rows, width), margin_table,
        vir_energy, vir_energy, amplitudes, k_term,
    )


def solution(mesh):
    placed = (
        P("pair", "aux", None),
        P("pair", "aux", None),
        P("pair", None, None),
        P("pair"),
        P("pair", "aux", None),
        P("pair", None),
        P(),
        P("pair", None),
    )
    return jax.shard_map(
        local, mesh=mesh, in_specs=placed, out_specs=P("pair", "aux", None), check_vma=False
    )
```

```python
import functools

import jax
import jax.numpy as jnp
from jax import lax
from jax.experimental import pallas as pl
from jax.experimental.pallas import tpu as pltpu
from jax.sharding import PartitionSpec as P

MESH = pl.DeviceIdType.MESH
VMEM_BYTES = 56 * 1024 * 1024
GROUP = 4
CHUNKS = 4
BLOCK = 16


def dot(a, b):
    return jnp.dot(a, b, preferred_element_type=jnp.float32)


def cycle_kernel(
    sizes, scale,
    last_ref, amp_hbm, fac_hbm, table_ref, cyc_out,
    amp, prefix, half, margin_t, both, r_send, r_own, r_recv, r_sum, r_in,
    f_plane, f_col, g_own, g_send, g_recv, c_own, c_send, c_recv, cyc,
    amp_sem, loc_sem, fp_s, fp_r, fz_s, fz_r, sr_s, sr_r, sg_s, sg_r, r_s, r_r, c_s, c_r,
    az_s, ap_s, ag_r,
):
    count, planes, cols, tables = sizes
    rows = amp.shape[1]
    pairs = amp.shape[0]
    me, h = lax.axis_index("pair"), lax.axis_index("aux")
    col, plane = lax.div(me, planes), lax.rem(me, planes)
    sibling = (me, 1 - h)
    plane_peers = [lax.rem(plane + d, planes) for d in range(1, planes)]
    col_peers = [lax.rem(col + d, cols) for d in range(1, cols)]

    def at_plane(t):
        return (col * planes + t, h)

    def at_col(z):
        return (z * planes + plane, h)

    def remote(src, dst, send, recv, device):
        return pltpu.make_async_remote_copy(
            src_ref=src, dst_ref=dst, send_sem=send, recv_sem=recv,
            device_id=device, device_id_type=MESH,
        )

    step = pairs // CHUNKS
    loads = []
    for k in range(CHUNKS):
        part = pl.ds(k * step, step)
        loads.append(pltpu.make_async_copy(amp_hbm.at[part], amp.at[part], amp_sem.at[k]))
        loads[-1].start()
    own_plane = pltpu.make_async_copy(fac_hbm.at[0], f_plane.at[plane], loc_sem.at[0])
    own_col = pltpu.make_async_copy(fac_hbm.at[0], f_col.at[col], loc_sem.at[1])
    own_plane.start()
    own_col.start()

    barrier = pltpu.get_barrier_semaphore()
    for device in [sibling] + [at_plane(t) for t in plane_peers] + [at_col(z) for z in col_peers]:
        pl.semaphore_signal(barrier, inc=1, device_id=device, device_id_type=MESH)
    pl.semaphore_wait(barrier, 1 + (planes - 1) + (cols - 1))

    sends = []
    for z in col_peers:
        sends.append(remote(fac_hbm.at[0], f_col.at[col], fz_s.at[z], fz_r.at[col], at_col(z)))
        sends[-1].start()
    for t in plane_peers:
        sends.append(remote(fac_hbm.at[0], f_plane.at[plane], fp_s.at[t], fp_r.at[plane], at_plane(t)))
        sends[-1].start()

    prefix[0] = jnp.zeros(prefix.shape[1:], jnp.float32)
    for m in range(tables):
        piece = table_ref[m, pl.ds(pl.multiple_of(h * rows, rows), rows), :]
        margin_t[:, m * rows : (m + 1) * rows] = piece.T
    both[0:rows] = margin_t[pl.ds(pl.multiple_of((1 - h) * rows, rows), rows), :]
    both[rows : 2 * rows] = margin_t[pl.ds(pl.multiple_of(h * rows, rows), rows), :]

    for k in range(CHUNKS):
        loads[k].wait()

        def add_pair(p, carry):
            prefix[p + 1] = amp[p].astype(jnp.float32) + prefix[last_ref[p]]
            return carry

        lax.fori_loop(k * step, (k + 1) * step, add_pair, 0, unroll=8)

    def rotate(base, held):
        for m in range(tables):
            found = [prefix[last_ref[pairs + (base + u) * tables + m]] for u in range(GROUP)]
            value = dot(jnp.concatenate(found, axis=0).astype(jnp.bfloat16), table_ref[m])
            value = value.astype(jnp.bfloat16)
            for u in range(GROUP):
                held[m * rows : (m + 1) * rows, u * 128 : (u + 1) * 128] = value[
                    u * rows : (u + 1) * rows
                ]
        for u in range(0, GROUP, 2):
            value = dot(both[...], held[:, u * 128 : (u + 2) * 128])
            for v in range(2):
                turned = value[:, v * 128 : (v + 1) * 128]
                r_send[base + u + v] = turned[0:rows].astype(jnp.bfloat16)
                r_own[base + u + v] = turned[rows : 2 * rows]

    def swap_piece(t):
        piece = pl.ds(t * cols, cols)
        return remote(r_send.at[piece], r_recv.at[piece], sr_s.at[t], sr_r.at[t], sibling)

    def add_piece(t):
        swap_piece(t).wait()
        piece = pl.ds(t * cols, cols)
        return (r_own[piece] + r_recv[piece].astype(jnp.float32)).astype(jnp.bfloat16)

    def send_piece(t):
        r_sum[t] = add_piece(t)
        sends.append(remote(r_sum.at[t], r_in.at[plane], r_s.at[t], r_r.at[plane], at_plane(t)))
        sends[-1].start()

    for d, t in enumerate(plane_peers + [plane]):
        held = half.at[d % 2]
        if cols == GROUP:
            rotate(t * cols, held)
        else:
            lax.fori_loop(
                0, cols // GROUP, lambda g, carry: rotate(t * cols + g * GROUP, held) or carry, 0
            )
        swap_piece(t).start()
        if d >= 1:
            send_piece(plane_peers[d - 1])

    own_plane.wait()
    own_col.wait()
    for t in plane_peers:
        remote(fac_hbm.at[0], f_plane.at[t], fp_s.at[t], fp_r.at[t], at_plane(t)).wait_recv()

    def swap_metric(z):
        return remote(g_send.at[z], g_recv.at[z], sg_s.at[z], sg_r.at[z], sibling)

    turned = [f_plane[s].T for s in range(planes)]
    for z in [col] + col_peers:
        if z is not col:
            remote(fac_hbm.at[0], f_col.at[z], fz_s.at[z], fz_r.at[z], at_col(z)).wait_recv()
        for s in range(planes):
            value = dot(turned[s], f_col[z])
            g_own[z, s * 128 : (s + 1) * 128, :] = value
            g_send[z, s * 128 : (s + 1) * 128, :] = value.astype(jnp.bfloat16)
        swap_metric(z).start()

    r_in[plane] = add_piece(plane)
    for t in plane_peers:
        remote(r_sum.at[t], r_in.at[t], r_s.at[t], r_r.at[t], at_plane(t)).wait_recv()

    for z in col_peers + [col]:
        swap_metric(z).wait()
        whole = (g_own[z] + g_recv[z].astype(jnp.float32)).astype(jnp.bfloat16)
        value = dot(jnp.concatenate([r_in[s, z] for s in range(planes)], axis=1), whole)
        if z is col:
            c_own[...] = value
        else:
            c_send[z] = value.astype(jnp.bfloat16)
            sends.append(remote(c_send.at[z], c_recv.at[col], c_s.at[z], c_r.at[col], at_col(z)))
            sends[-1].start()
    total = c_own[...]
    for z in col_peers:
        remote(c_send.at[z], c_recv.at[z], c_s.at[z], c_r.at[z], at_col(z)).wait_recv()
        total = total + c_recv[z].astype(jnp.float32)
    cyc[col, plane] = (scale * total).astype(jnp.bfloat16)

    mine_cyc = cyc.at[col, plane]
    for z in col_peers:
        sends.append(remote(mine_cyc, mine_cyc, az_s.at[z], ag_r.at[col, plane], at_col(z)))
        sends[-1].start()
    for t in plane_peers:
        sends.append(remote(mine_cyc, mine_cyc, ap_s.at[col, t], ag_r.at[col, plane], at_plane(t)))
        sends[-1].start()
    for z in col_peers:
        block = cyc.at[z, plane]
        remote(block, block, az_s.at[z], ag_r.at[z, plane], at_col(z)).wait_recv()
        for t in plane_peers:
            sends.append(remote(block, block, ap_s.at[z, t], ag_r.at[z, plane], at_plane(t)))
            sends[-1].start()
    for t in plane_peers:
        for z in [col] + col_peers:
            block = cyc.at[z, t]
            remote(block, block, ap_s.at[z, t], ag_r.at[z, t], at_plane(t)).wait_recv()
    cyc_out[...] = cyc[...]
    for copy in sends:
        copy.wait_send()


def update_kernel(
    margin_ref, owner_ref, occ_ref, cyc_ref, table_ref, energy_ref, amp_hbm, k_hbm,
    out_hbm, term, energy_t, amp, k_held, out, amp_sem, k_sem, out_sem,
):
    tables, count = term.shape[0], term.shape[1]
    pairs, rows = amp.shape[0], amp.shape[1]
    first = occ_ref[lax.axis_index("pair")]
    h = lax.axis_index("aux")

    def load(s):
        part = pl.ds(s * BLOCK, BLOCK)
        return (
            pltpu.make_async_copy(amp_hbm.at[part], amp.at[part], amp_sem.at[s]),
            pltpu.make_async_copy(k_hbm.at[part], k_held.at[part], k_sem.at[s]),
        )

    def store(s):
        part = pl.ds(s * BLOCK, BLOCK)
        return pltpu.make_async_copy(out.at[part], out_hbm.at[part], out_sem.at[s])

    for s in range(pairs // BLOCK):
        for copy in load(s):
            copy.start()

    energy_t[...] = energy_ref[...].T

    def form(g, carry):
        at = pl.multiple_of(g * 8, 8)
        left = cyc_ref[pl.ds(at, 8)].reshape(8 * rows, 128)
        for m in range(0, tables, 2):
            right = table_ref[m : m + 2].reshape(256, 128)
            value = lax.dot_general(
                left, right, (((1,), (1,)), ((), ())), preferred_element_type=jnp.float32
            )
            for v in range(2):
                term[m + v, pl.ds(at, 8)] = value[:, v * 128 : (v + 1) * 128].reshape(8, rows, 128)
        return carry

    lax.fori_loop(0, count // 8, form, 0)

    def renew(s, carry):
        for copy in load(s):
            copy.wait()
        mine = energy_t[pl.ds(pl.multiple_of(h * rows, rows), rows), :]
        mine = pltpu.roll(mine, lax.rem(pairs - s * BLOCK, pairs), 1)
        for u in range(BLOCK):
            p = s * BLOCK + u
            owner = owner_ref[p]
            across = energy_ref[pl.ds(p, 1), :] - (first + occ_ref[owner])
            denominator = mine[:, u : u + 1] + across
            inverse = pl.reciprocal(denominator, approx=True)
            inverse = inverse * (2.0 - denominator * inverse)
            numerator = term[margin_ref[p], owner] + k_held[p].astype(jnp.float32)
            out[p] = (amp[p].astype(jnp.float32) - numerator * inverse).astype(jnp.bfloat16)
        store(s).start()
        return carry

    lax.fori_loop(0, pairs // BLOCK, renew, 0)
    for s in range(pairs // BLOCK):
        store(s).wait()


def local(
    amplitudes, k_term, margin_table, margin_index, factors, vir_energy, occ_energy, pair_owner
):
    count = lax.axis_size("pair")
    aux_count = lax.axis_size("aux")
    pairs, rows, width = amplitudes.shape
    aux_rows = factors.shape[1]
    tables = margin_table.shape[0]
    planes = 4
    cols = count // planes
    scale = float(width * aux_rows * aux_count * pairs) ** (-0.5)
    bf16, f32 = jnp.bfloat16, jnp.float32

    owner = pair_owner[:, 0]
    slot = (owner % planes) * cols + owner // planes
    key = slot * tables + margin_index
    place = jnp.arange(pairs, dtype=jnp.int32)
    sought = jnp.concatenate([key, jnp.arange(count * tables, dtype=jnp.int32)])
    bound = jnp.concatenate([place, jnp.full((count * tables,), pairs, jnp.int32)])
    hit = (key[None, :] == sought[:, None]) & (place[None, :] < bound[:, None])
    last = jnp.max(jnp.where(hit, place[None, :] + 1, 0), axis=1)

    dma = pltpu.SemaphoreType.DMA
    vmem = pl.BlockSpec(memory_space=pltpu.VMEM)
    smem = pl.BlockSpec(memory_space=pltpu.SMEM)
    anywhere = pl.BlockSpec(memory_space=pl.ANY)
    cyc = pl.pallas_call(
        functools.partial(cycle_kernel, (count, planes, cols, tables), scale),
        out_shape=jax.ShapeDtypeStruct((cols, planes, rows, width), bf16),
        in_specs=[smem, anywhere, anywhere, vmem],
        out_specs=vmem,
        scratch_shapes=[
            pltpu.VMEM((pairs, rows, width), bf16),
            pltpu.VMEM((pairs + 1, rows, width), f32),
            pltpu.VMEM((2, tables * rows, GROUP * width), bf16),
            pltpu.VMEM((width, tables * rows), bf16),
            pltpu.VMEM((2 * rows, tables * rows), bf16),
            pltpu.VMEM((count, rows, width), bf16),
            pltpu.VMEM((count, rows, width), f32),
            pltpu.VMEM((count, rows, width), bf16),
            pltpu.VMEM((planes, cols, rows, width), bf16),
            pltpu.VMEM((planes, cols, rows, width), bf16),
            pltpu.VMEM((planes, aux_rows, width), bf16),
            pltpu.VMEM((cols, aux_rows, width), bf16),
            pltpu.VMEM((cols, planes * width, width), f32),
            pltpu.VMEM((cols, planes * width, width), bf16),
            pltpu.VMEM((cols, planes * width, width), bf16),
            pltpu.VMEM((rows, width), f32),
            pltpu.VMEM((cols, rows, width), bf16),
            pltpu.VMEM((cols, rows, width), bf16),
            pltpu.VMEM((cols, planes, rows, width), bf16),
            dma((CHUNKS,)),
            dma((2,)),
            dma((planes,)),
            dma((planes,)),
            dma((cols,)),
            dma((cols,)),
            dma((planes,)),
            dma((planes,)),
            dma((cols,)),
            dma((cols,)),
            dma((planes,)),
            dma((planes,)),
            dma((cols,)),
            dma((cols,)),
            dma((cols,)),
            dma((cols, planes)),
            dma((cols, planes)),
        ],
        compiler_params=pltpu.CompilerParams(
            collective_id=0, has_side_effects=True, vmem_limit_bytes=VMEM_BYTES
        ),
        name="cycle",
    )(last, amplitudes, factors, margin_table)

    whole = pltpu.VMEM((pairs, rows, width), bf16)
    return pl.pallas_call(
        update_kernel,
        out_shape=jax.ShapeDtypeStruct(amplitudes.shape, bf16),
        in_specs=[smem, smem, smem, vmem, vmem, vmem, anywhere, anywhere],
        out_specs=anywhere,
        scratch_shapes=[
            pltpu.VMEM((tables, count, rows, width), f32),
            pltpu.VMEM((width, pairs), f32),
            whole,
            whole,
            whole,
            dma((pairs // BLOCK,)),
            dma((pairs // BLOCK,)),
            dma((pairs // BLOCK,)),
        ],
        compiler_params=pltpu.CompilerParams(vmem_limit_bytes=VMEM_BYTES),
        name="update",
    )(
        margin_index, owner, occ_energy, cyc.reshape(count, rows, width), margin_table,
        vir_energy, amplitudes, k_term,
    )


def solution(mesh):
    placed = (
        P("pair", "aux", None),
        P("pair", "aux", None),
        P("pair", None, None),
        P("pair"),
        P("pair", "aux", None),
        P("pair", None),
        P(),
        P("pair", None),
    )
    return jax.shard_map(
        local, mesh=mesh, in_specs=placed, out_specs=P("pair", "aux", None), check_vma=False
    )
```

```python
import functools

import jax
import jax.numpy as jnp
from jax import lax
from jax.experimental import pallas as pl
from jax.experimental.pallas import tpu as pltpu
from jax.sharding import PartitionSpec as P

MESH = pl.DeviceIdType.MESH
GROUP = 4
CHUNKS = 4
BLOCK = 16


def dot(a, b):
    return jnp.dot(a, b, preferred_element_type=jnp.float32)


def cycle_kernel(
    sizes, scale,
    last_ref, amp_hbm, fac_hbm, table_ref, cyc_out,
    amp, prefix, half, margin_t, both, r_send, r_own, r_recv, r_sum, r_in,
    f_plane, f_col, g_own, g_send, g_recv, c_own, c_send, c_recv, cyc,
    amp_sem, loc_sem, fp_s, fp_r, fz_s, fz_r, sr_s, sr_r, sg_s, sg_r, r_s, r_r, c_s, c_r,
    az_s, ap_s, ag_r,
):
    count, planes, cols, tables = sizes
    rows = amp.shape[1]
    pairs = amp.shape[0]
    me, h = lax.axis_index("pair"), lax.axis_index("aux")
    col, plane = lax.div(me, planes), lax.rem(me, planes)
    sibling = (me, 1 - h)
    plane_peers = [lax.rem(plane + d, planes) for d in range(1, planes)]
    col_peers = [lax.rem(col + d, cols) for d in range(1, cols)]

    def at_plane(t):
        return (col * planes + t, h)

    def at_col(z):
        return (z * planes + plane, h)

    def remote(src, dst, send, recv, device):
        return pltpu.make_async_remote_copy(
            src_ref=src, dst_ref=dst, send_sem=send, recv_sem=recv,
            device_id=device, device_id_type=MESH,
        )

    step = pairs // CHUNKS
    loads = []
    for k in range(CHUNKS):
        part = pl.ds(k * step, step)
        loads.append(pltpu.make_async_copy(amp_hbm.at[part], amp.at[part], amp_sem.at[k]))
        loads[-1].start()
    own_plane = pltpu.make_async_copy(fac_hbm.at[0], f_plane.at[plane], loc_sem.at[0])
    own_col = pltpu.make_async_copy(fac_hbm.at[0], f_col.at[col], loc_sem.at[1])
    own_plane.start()
    own_col.start()

    barrier = pltpu.get_barrier_semaphore()
    for device in [sibling] + [at_plane(t) for t in plane_peers] + [at_col(z) for z in col_peers]:
        pl.semaphore_signal(barrier, inc=1, device_id=device, device_id_type=MESH)
    pl.semaphore_wait(barrier, 1 + (planes - 1) + (cols - 1))

    sends = []
    for z in col_peers:
        sends.append(remote(fac_hbm.at[0], f_col.at[col], fz_s.at[z], fz_r.at[col], at_col(z)))
        sends[-1].start()
    for t in plane_peers:
        sends.append(remote(fac_hbm.at[0], f_plane.at[plane], fp_s.at[t], fp_r.at[plane], at_plane(t)))
        sends[-1].start()

    prefix[0] = jnp.zeros(prefix.shape[1:], jnp.float32)
    for m in range(tables):
        piece = table_ref[m, pl.ds(pl.multiple_of(h * rows, rows), rows), :]
        margin_t[:, m * rows : (m + 1) * rows] = piece.T
    both[0:rows] = margin_t[pl.ds(pl.multiple_of((1 - h) * rows, rows), rows), :]
    both[rows : 2 * rows] = margin_t[pl.ds(pl.multiple_of(h * rows, rows), rows), :]

    for k in range(CHUNKS):
        loads[k].wait()

        def add_pair(p, carry):
            prefix[p + 1] = amp[p].astype(jnp.float32) + prefix[last_ref[p]]
            return carry

        lax.fori_loop(k * step, (k + 1) * step, add_pair, 0, unroll=8)

    def rotate(base, held):
        for m in range(tables):
            found = [prefix[last_ref[pairs + (base + u) * tables + m]] for u in range(GROUP)]
            value = dot(jnp.concatenate(found, axis=0).astype(jnp.bfloat16), table_ref[m])
            value = value.astype(jnp.bfloat16)
            for u in range(GROUP):
                held[m * rows : (m + 1) * rows, u * 128 : (u + 1) * 128] = value[
                    u * rows : (u + 1) * rows
                ]
        for u in range(0, GROUP, 2):
            value = dot(both[...], held[:, u * 128 : (u + 2) * 128])
            for v in range(2):
                turned = value[:, v * 128 : (v + 1) * 128]
                r_send[base + u + v] = turned[0:rows].astype(jnp.bfloat16)
                r_own[base + u + v] = turned[rows : 2 * rows]

    def swap_piece(t):
        piece = pl.ds(t * cols, cols)
        return remote(r_send.at[piece], r_recv.at[piece], sr_s.at[t], sr_r.at[t], sibling)

    def add_piece(t):
        swap_piece(t).wait()
        piece = pl.ds(t * cols, cols)
        return (r_own[piece] + r_recv[piece].astype(jnp.float32)).astype(jnp.bfloat16)

    def send_piece(t):
        r_sum[t] = add_piece(t)
        sends.append(remote(r_sum.at[t], r_in.at[plane], r_s.at[t], r_r.at[plane], at_plane(t)))
        sends[-1].start()

    def rotate_all(d, t):
        held = half.at[d % 2]
        if cols == GROUP:
            rotate(t * cols, held)
        else:
            lax.fori_loop(
                0, cols // GROUP, lambda g, carry: rotate(t * cols + g * GROUP, held) or carry, 0
            )
        swap_piece(t).start()

    for d, t in enumerate(plane_peers):
        rotate_all(d, t)
        if d >= 1:
            send_piece(plane_peers[d - 1])

    own_plane.wait()
    own_col.wait()
    for t in plane_peers:
        remote(fac_hbm.at[0], f_plane.at[t], fp_s.at[t], fp_r.at[t], at_plane(t)).wait_recv()

    def swap_metric(z):
        return remote(g_send.at[z], g_recv.at[z], sg_s.at[z], sg_r.at[z], sibling)

    turned = [f_plane[s].T for s in range(planes)]
    for z in [col] + col_peers:
        if z is not col:
            remote(fac_hbm.at[0], f_col.at[z], fz_s.at[z], fz_r.at[z], at_col(z)).wait_recv()
        for s in range(planes):
            value = dot(turned[s], f_col[z])
            g_own[z, s * 128 : (s + 1) * 128, :] = value
            g_send[z, s * 128 : (s + 1) * 128, :] = value.astype(jnp.bfloat16)
        swap_metric(z).start()
        if z is col:
            send_piece(plane_peers[-1])

    rotate_all(planes - 1, plane)
    r_in[plane] = add_piece(plane)
    for t in plane_peers:
        remote(r_sum.at[t], r_in.at[t], r_s.at[t], r_r.at[t], at_plane(t)).wait_recv()

    for z in col_peers + [col]:
        swap_metric(z).wait()
        whole = (g_own[z] + g_recv[z].astype(jnp.float32)).astype(jnp.bfloat16)
        value = dot(jnp.concatenate([r_in[s, z] for s in range(planes)], axis=1), whole)
        if z is col:
            c_own[...] = value
        else:
            c_send[z] = value.astype(jnp.bfloat16)
            sends.append(remote(c_send.at[z], c_recv.at[col], c_s.at[z], c_r.at[col], at_col(z)))
            sends[-1].start()
    total = c_own[...]
    for z in col_peers:
        remote(c_send.at[z], c_recv.at[z], c_s.at[z], c_r.at[z], at_col(z)).wait_recv()
        total = total + c_recv[z].astype(jnp.float32)
    cyc[col, plane] = (scale * total).astype(jnp.bfloat16)

    mine_cyc = cyc.at[col, plane]
    for z in col_peers:
        sends.append(remote(mine_cyc, mine_cyc, az_s.at[z], ag_r.at[col, plane], at_col(z)))
        sends[-1].start()
    for t in plane_peers:
        sends.append(remote(mine_cyc, mine_cyc, ap_s.at[col, t], ag_r.at[col, plane], at_plane(t)))
        sends[-1].start()
    for z in col_peers:
        block = cyc.at[z, plane]
        remote(block, block, az_s.at[z], ag_r.at[z, plane], at_col(z)).wait_recv()
        for t in plane_peers:
            sends.append(remote(block, block, ap_s.at[z, t], ag_r.at[z, plane], at_plane(t)))
            sends[-1].start()
    for t in plane_peers:
        for z in [col] + col_peers:
            block = cyc.at[z, t]
            remote(block, block, ap_s.at[z, t], ag_r.at[z, t], at_plane(t)).wait_recv()
    cyc_out[...] = cyc[...]
    for copy in sends:
        copy.wait_send()


def update_kernel(
    margin_ref, owner_ref, occ_ref, cyc_ref, table_ref, energy_ref, amp_hbm, k_hbm,
    out_hbm, term, energy_t, amp, k_held, out, amp_sem, k_sem, out_sem,
):
    tables, count = term.shape[0], term.shape[1]
    pairs, rows = amp.shape[0], amp.shape[1]
    first = occ_ref[lax.axis_index("pair")]
    h = lax.axis_index("aux")

    def load(s):
        part = pl.ds(s * BLOCK, BLOCK)
        return (
            pltpu.make_async_copy(amp_hbm.at[part], amp.at[part], amp_sem.at[s]),
            pltpu.make_async_copy(k_hbm.at[part], k_held.at[part], k_sem.at[s]),
        )

    def store(s):
        part = pl.ds(s * BLOCK, BLOCK)
        return pltpu.make_async_copy(out.at[part], out_hbm.at[part], out_sem.at[s])

    for s in range(pairs // BLOCK):
        for copy in load(s):
            copy.start()

    energy_t[...] = energy_ref[...].T

    def form(g, carry):
        at = pl.multiple_of(g * 8, 8)
        left = cyc_ref[pl.ds(at, 8)].reshape(8 * rows, 128)
        for m in range(0, tables, 2):
            right = table_ref[m : m + 2].reshape(256, 128)
            value = lax.dot_general(
                left, right, (((1,), (1,)), ((), ())), preferred_element_type=jnp.float32
            )
            for v in range(2):
                term[m + v, pl.ds(at, 8)] = value[:, v * 128 : (v + 1) * 128].reshape(8, rows, 128)
        return carry

    lax.fori_loop(0, count // 8, form, 0)

    def renew(s, carry):
        for copy in load(s):
            copy.wait()
        mine = energy_t[pl.ds(pl.multiple_of(h * rows, rows), rows), :]
        mine = pltpu.roll(mine, lax.rem(pairs - s * BLOCK, pairs), 1)
        for u in range(BLOCK):
            p = s * BLOCK + u
            owner = owner_ref[p]
            across = energy_ref[pl.ds(p, 1), :] - (first + occ_ref[owner])
            denominator = mine[:, u : u + 1] + across
            inverse = pl.reciprocal(denominator, approx=True)
            inverse = inverse * (2.0 - denominator * inverse)
            numerator = term[margin_ref[p], owner] + k_held[p].astype(jnp.float32)
            out[p] = (amp[p].astype(jnp.float32) - numerator * inverse).astype(jnp.bfloat16)
        store(s).start()
        return carry

    lax.fori_loop(0, pairs // BLOCK, renew, 0)
    for s in range(pairs // BLOCK):
        store(s).wait()


def local(
    amplitudes, k_term, margin_table, margin_index, factors, vir_energy, occ_energy, pair_owner
):
    count = lax.axis_size("pair")
    aux_count = lax.axis_size("aux")
    pairs, rows, width = amplitudes.shape
    aux_rows = factors.shape[1]
    tables = margin_table.shape[0]
    planes = 4
    cols = count // planes
    scale = float(width * aux_rows * aux_count * pairs) ** (-0.5)
    bf16, f32 = jnp.bfloat16, jnp.float32
    vmem_bytes = min(56 << 20, (14 << 20) + count * (3 << 17))

    owner = pair_owner[:, 0]
    slot = (owner % planes) * cols + owner // planes
    key = slot * tables + margin_index
    place = jnp.arange(pairs, dtype=jnp.int32)
    sought = jnp.concatenate([key, jnp.arange(count * tables, dtype=jnp.int32)])
    bound = jnp.concatenate([place, jnp.full((count * tables,), pairs, jnp.int32)])
    hit = (key[:, None] == sought[None, :]) & (place[:, None] < bound[None, :])
    last = jnp.max(jnp.where(hit, place[:, None] + 1, 0), axis=0)

    dma = pltpu.SemaphoreType.DMA
    vmem = pl.BlockSpec(memory_space=pltpu.VMEM)
    smem = pl.BlockSpec(memory_space=pltpu.SMEM)
    anywhere = pl.BlockSpec(memory_space=pl.ANY)
    cyc = pl.pallas_call(
        functools.partial(cycle_kernel, (count, planes, cols, tables), scale),
        out_shape=jax.ShapeDtypeStruct((cols, planes, rows, width), bf16),
        in_specs=[smem, anywhere, anywhere, vmem],
        out_specs=vmem,
        scratch_shapes=[
            pltpu.VMEM((pairs, rows, width), bf16),
            pltpu.VMEM((pairs + 1, rows, width), f32),
            pltpu.VMEM((2, tables * rows, GROUP * width), bf16),
            pltpu.VMEM((width, tables * rows), bf16),
            pltpu.VMEM((2 * rows, tables * rows), bf16),
            pltpu.VMEM((count, rows, width), bf16),
            pltpu.VMEM((count, rows, width), f32),
            pltpu.VMEM((count, rows, width), bf16),
            pltpu.VMEM((planes, cols, rows, width), bf16),
            pltpu.VMEM((planes, cols, rows, width), bf16),
            pltpu.VMEM((planes, aux_rows, width), bf16),
            pltpu.VMEM((cols, aux_rows, width), bf16),
            pltpu.VMEM((cols, planes * width, width), f32),
            pltpu.VMEM((cols, planes * width, width), bf16),
            pltpu.VMEM((cols, planes * width, width), bf16),
            pltpu.VMEM((rows, width), f32),
            pltpu.VMEM((cols, rows, width), bf16),
            pltpu.VMEM((cols, rows, width), bf16),
            pltpu.VMEM((cols, planes, rows, width), bf16),
            dma((CHUNKS,)),
            dma((2,)),
            dma((planes,)),
            dma((planes,)),
            dma((cols,)),
            dma((cols,)),
            dma((planes,)),
            dma((planes,)),
            dma((cols,)),
            dma((cols,)),
            dma((planes,)),
            dma((planes,)),
            dma((cols,)),
            dma((cols,)),
            dma((cols,)),
            dma((cols, planes)),
            dma((cols, planes)),
        ],
        compiler_params=pltpu.CompilerParams(
            collective_id=0, has_side_effects=True, vmem_limit_bytes=vmem_bytes
        ),
        name="cycle",
    )(last, amplitudes, factors, margin_table)

    whole = pltpu.VMEM((pairs, rows, width), bf16)
    return pl.pallas_call(
        update_kernel,
        out_shape=jax.ShapeDtypeStruct(amplitudes.shape, bf16),
        in_specs=[smem, smem, smem, vmem, vmem, vmem, anywhere, anywhere],
        out_specs=anywhere,
        scratch_shapes=[
            pltpu.VMEM((tables, count, rows, width), f32),
            pltpu.VMEM((width, pairs), f32),
            whole,
            whole,
            whole,
            dma((pairs // BLOCK,)),
            dma((pairs // BLOCK,)),
            dma((pairs // BLOCK,)),
        ],
        compiler_params=pltpu.CompilerParams(vmem_limit_bytes=vmem_bytes),
        name="update",
    )(
        margin_index, owner, occ_energy, cyc.reshape(count, rows, width), margin_table,
        vir_energy, amplitudes, k_term,
    )


def solution(mesh):
    placed = (
        P("pair", "aux", None),
        P("pair", "aux", None),
        P("pair", None, None),
        P("pair"),
        P("pair", "aux", None),
        P("pair", None),
        P(),
        P("pair", None),
    )
    return jax.shard_map(
        local, mesh=mesh, in_specs=placed, out_specs=P("pair", "aux", None), check_vma=False
    )
```

```python
import functools

import jax
import jax.numpy as jnp
from jax import lax
from jax.experimental import pallas as pl
from jax.experimental.pallas import tpu as pltpu
from jax.sharding import PartitionSpec as P

MESH = pl.DeviceIdType.MESH
GROUP = 4
CHUNKS = 4
BLOCK = 16


def dot(a, b):
    return jnp.dot(a, b, preferred_element_type=jnp.float32)


def cycle_kernel(
    sizes, scale,
    last_ref, amp_hbm, fac_hbm, table_ref, cyc_out,
    amp, prefix, half, margin_t, both, r_send, r_own, r_recv, r_sum, r_in,
    f_plane, f_col, g_own, g_send, g_recv, c_own, c_send, c_recv, cyc,
    amp_sem, loc_sem, fp_s, fp_r, fz_s, fz_r, sr_s, sr_r, sg_s, sg_r, r_s, r_r, c_s, c_r,
    az_s, ap_s, ag_r,
):
    count, planes, cols, tables = sizes
    rows = amp.shape[1]
    pairs = amp.shape[0]
    me, h = lax.axis_index("pair"), lax.axis_index("aux")
    col, plane = lax.div(me, planes), lax.rem(me, planes)
    sibling = (me, 1 - h)
    plane_peers = [lax.rem(plane + d, planes) for d in range(1, planes)]
    col_peers = [lax.rem(col + d, cols) for d in range(1, cols)]

    def at_plane(t):
        return (col * planes + t, h)

    def at_col(z):
        return (z * planes + plane, h)

    def remote(src, dst, send, recv, device):
        return pltpu.make_async_remote_copy(
            src_ref=src, dst_ref=dst, send_sem=send, recv_sem=recv,
            device_id=device, device_id_type=MESH,
        )

    step = pairs // CHUNKS
    loads = []
    for k in range(CHUNKS):
        part = pl.ds(k * step, step)
        loads.append(pltpu.make_async_copy(amp_hbm.at[part], amp.at[part], amp_sem.at[k]))
        loads[-1].start()
    own_plane = pltpu.make_async_copy(fac_hbm.at[0], f_plane.at[plane], loc_sem.at[0])
    own_col = pltpu.make_async_copy(fac_hbm.at[0], f_col.at[col], loc_sem.at[1])
    own_plane.start()
    own_col.start()

    barrier = pltpu.get_barrier_semaphore()
    for device in [sibling] + [at_plane(t) for t in plane_peers] + [at_col(z) for z in col_peers]:
        pl.semaphore_signal(barrier, inc=1, device_id=device, device_id_type=MESH)
    pl.semaphore_wait(barrier, 1 + (planes - 1) + (cols - 1))

    sends = []
    for z in col_peers:
        sends.append(remote(fac_hbm.at[0], f_col.at[col], fz_s.at[z], fz_r.at[col], at_col(z)))
        sends[-1].start()
    for t in plane_peers:
        sends.append(remote(fac_hbm.at[0], f_plane.at[plane], fp_s.at[t], fp_r.at[plane], at_plane(t)))
        sends[-1].start()

    prefix[0] = jnp.zeros(prefix.shape[1:], jnp.float32)
    for m in range(tables):
        piece = table_ref[m, pl.ds(pl.multiple_of(h * rows, rows), rows), :]
        margin_t[:, m * rows : (m + 1) * rows] = piece.T
    both[0:rows] = margin_t[pl.ds(pl.multiple_of((1 - h) * rows, rows), rows), :]
    both[rows : 2 * rows] = margin_t[pl.ds(pl.multiple_of(h * rows, rows), rows), :]

    for k in range(CHUNKS):
        loads[k].wait()

        def add_pair(p, carry):
            prefix[p + 1] = amp[p].astype(jnp.float32) + prefix[last_ref[p]]
            return carry

        lax.fori_loop(k * step, (k + 1) * step, add_pair, 0, unroll=8)

    def rotate(base, held):
        for m in range(tables):
            found = [prefix[last_ref[pairs + (base + u) * tables + m]] for u in range(GROUP)]
            value = dot(jnp.concatenate(found, axis=0).astype(jnp.bfloat16), table_ref[m])
            value = value.astype(jnp.bfloat16)
            for u in range(GROUP):
                held[m * rows : (m + 1) * rows, u * 128 : (u + 1) * 128] = value[
                    u * rows : (u + 1) * rows
                ]
        for u in range(0, GROUP, 2):
            value = dot(both[...], held[:, u * 128 : (u + 2) * 128])
            for v in range(2):
                turned = value[:, v * 128 : (v + 1) * 128]
                r_send[base + u + v] = turned[0:rows].astype(jnp.bfloat16)
                r_own[base + u + v] = turned[rows : 2 * rows]

    def swap_piece(t):
        piece = pl.ds(t * cols, cols)
        return remote(r_send.at[piece], r_recv.at[piece], sr_s.at[t], sr_r.at[t], sibling)

    def add_piece(t):
        swap_piece(t).wait()
        piece = pl.ds(t * cols, cols)
        return (r_own[piece] + r_recv[piece].astype(jnp.float32)).astype(jnp.bfloat16)

    def send_piece(t):
        r_sum[t] = add_piece(t)
        sends.append(remote(r_sum.at[t], r_in.at[plane], r_s.at[t], r_r.at[plane], at_plane(t)))
        sends[-1].start()

    def rotate_all(d, t):
        held = half.at[d % 2]
        if cols == GROUP:
            rotate(t * cols, held)
        else:
            lax.fori_loop(
                0, cols // GROUP, lambda g, carry: rotate(t * cols + g * GROUP, held) or carry, 0
            )
        swap_piece(t).start()

    for d, t in enumerate(plane_peers):
        rotate_all(d, t)
        if d >= 1:
            send_piece(plane_peers[d - 1])

    own_plane.wait()
    own_col.wait()
    for t in plane_peers:
        remote(fac_hbm.at[0], f_plane.at[t], fp_s.at[t], fp_r.at[t], at_plane(t)).wait_recv()

    def swap_metric(z):
        return remote(g_send.at[z], g_recv.at[z], sg_s.at[z], sg_r.at[z], sibling)

    turned = [f_plane[s].T for s in range(planes)]
    for z in [col] + col_peers:
        if z is not col:
            remote(fac_hbm.at[0], f_col.at[z], fz_s.at[z], fz_r.at[z], at_col(z)).wait_recv()
        for s in range(planes):
            value = dot(turned[s], f_col[z])
            g_own[z, s * 128 : (s + 1) * 128, :] = value
            g_send[z, s * 128 : (s + 1) * 128, :] = value.astype(jnp.bfloat16)
        swap_metric(z).start()
        if z is col:
            send_piece(plane_peers[-1])

    rotate_all(planes - 1, plane)
    r_in[plane] = add_piece(plane)
    for t in plane_peers:
        remote(r_sum.at[t], r_in.at[t], r_s.at[t], r_r.at[t], at_plane(t)).wait_recv()

    for z in col_peers + [col]:
        swap_metric(z).wait()
        whole = (g_own[z] + g_recv[z].astype(jnp.float32)).astype(jnp.bfloat16)
        value = dot(jnp.concatenate([r_in[s, z] for s in range(planes)], axis=1), whole)
        if z is col:
            c_own[...] = value
        else:
            c_send[z] = value.astype(jnp.bfloat16)
            sends.append(remote(c_send.at[z], c_recv.at[col], c_s.at[z], c_r.at[col], at_col(z)))
            sends[-1].start()
    total = c_own[...]
    for z in col_peers:
        remote(c_send.at[z], c_recv.at[z], c_s.at[z], c_r.at[z], at_col(z)).wait_recv()
        total = total + c_recv[z].astype(jnp.float32)
    cyc[col, plane] = (scale * total).astype(jnp.bfloat16)

    mine_cyc = cyc.at[col, plane]
    for z in col_peers:
        sends.append(remote(mine_cyc, mine_cyc, az_s.at[z], ag_r.at[col, plane], at_col(z)))
        sends[-1].start()
    for t in plane_peers:
        sends.append(remote(mine_cyc, mine_cyc, ap_s.at[col, t], ag_r.at[col, plane], at_plane(t)))
        sends[-1].start()
    for z in col_peers:
        block = cyc.at[z, plane]
        remote(block, block, az_s.at[z], ag_r.at[z, plane], at_col(z)).wait_recv()
        for t in plane_peers:
            sends.append(remote(block, block, ap_s.at[z, t], ag_r.at[z, plane], at_plane(t)))
            sends[-1].start()
    for t in plane_peers:
        for z in [col] + col_peers:
            block = cyc.at[z, t]
            remote(block, block, ap_s.at[z, t], ag_r.at[z, t], at_plane(t)).wait_recv()
    cyc_out[...] = cyc[...]
    for copy in sends:
        copy.wait_send()


def update_kernel(
    margin_ref, owner_ref, occ_ref, cyc_ref, table_ref, energy_ref, amp_hbm, k_hbm,
    out_hbm, term, energy_t, amp, k_held, out, amp_sem, k_sem, out_sem,
):
    tables, count = term.shape[0], term.shape[1]
    pairs, rows = amp.shape[0], amp.shape[1]
    first = occ_ref[lax.axis_index("pair")]
    h = lax.axis_index("aux")

    def load(s):
        part = pl.ds(s * BLOCK, BLOCK)
        return (
            pltpu.make_async_copy(amp_hbm.at[part], amp.at[part], amp_sem.at[s]),
            pltpu.make_async_copy(k_hbm.at[part], k_held.at[part], k_sem.at[s]),
        )

    def store(s):
        part = pl.ds(s * BLOCK, BLOCK)
        return pltpu.make_async_copy(out.at[part], out_hbm.at[part], out_sem.at[s])

    for s in range(pairs // BLOCK):
        for copy in load(s):
            copy.start()

    energy_t[...] = energy_ref[...].T

    def form(g, carry):
        at = pl.multiple_of(g * 8, 8)
        left = cyc_ref[pl.ds(at, 8)].reshape(8 * rows, 128)
        for m in range(0, tables, 2):
            right = table_ref[m : m + 2].reshape(256, 128)
            value = lax.dot_general(
                left, right, (((1,), (1,)), ((), ())), preferred_element_type=jnp.float32
            )
            for v in range(2):
                term[m + v, pl.ds(at, 8)] = value[:, v * 128 : (v + 1) * 128].reshape(8, rows, 128)
        return carry

    lax.fori_loop(0, count // 8, form, 0)

    def renew(s, carry):
        for copy in load(s):
            copy.wait()
        mine = energy_t[pl.ds(pl.multiple_of(h * rows, rows), rows), :]
        mine = pltpu.roll(mine, lax.rem(pairs - s * BLOCK, pairs), 1)
        for u in range(BLOCK):
            p = s * BLOCK + u
            owner = owner_ref[p]
            across = energy_ref[pl.ds(p, 1), :] - (first + occ_ref[owner])
            denominator = mine[:, u : u + 1] + across
            inverse = pl.reciprocal(denominator, approx=True)
            inverse = inverse * (2.0 - denominator * inverse)
            numerator = term[margin_ref[p], owner] + k_held[p].astype(jnp.float32)
            out[p] = (amp[p].astype(jnp.float32) - numerator * inverse).astype(jnp.bfloat16)
        store(s).start()
        return carry

    lax.fori_loop(0, pairs // BLOCK, renew, 0)
    for s in range(pairs // BLOCK):
        store(s).wait()


def local(
    amplitudes, k_term, margin_table, margin_index, factors, vir_energy, occ_energy, pair_owner
):
    count = lax.axis_size("pair")
    aux_count = lax.axis_size("aux")
    pairs, rows, width = amplitudes.shape
    aux_rows = factors.shape[1]
    tables = margin_table.shape[0]
    planes = 4
    cols = count // planes
    scale = float(width * aux_rows * aux_count * pairs) ** (-0.5)
    bf16, f32 = jnp.bfloat16, jnp.float32
    vmem_bytes = 56 << 20

    owner = pair_owner[:, 0]
    slot = (owner % planes) * cols + owner // planes
    key = slot * tables + margin_index
    place = jnp.arange(pairs, dtype=jnp.int32)
    sought = jnp.concatenate([key, jnp.arange(count * tables, dtype=jnp.int32)])
    bound = jnp.concatenate([place, jnp.full((count * tables,), pairs, jnp.int32)])
    hit = (key[:, None] == sought[None, :]) & (place[:, None] < bound[None, :])
    last = jnp.max(jnp.where(hit, place[:, None] + 1, 0), axis=0)

    dma = pltpu.SemaphoreType.DMA
    vmem = pl.BlockSpec(memory_space=pltpu.VMEM)
    smem = pl.BlockSpec(memory_space=pltpu.SMEM)
    anywhere = pl.BlockSpec(memory_space=pl.ANY)
    cyc = pl.pallas_call(
        functools.partial(cycle_kernel, (count, planes, cols, tables), scale),
        out_shape=jax.ShapeDtypeStruct((cols, planes, rows, width), bf16),
        in_specs=[smem, anywhere, anywhere, vmem],
        out_specs=vmem,
        scratch_shapes=[
            pltpu.VMEM((pairs, rows, width), bf16),
            pltpu.VMEM((pairs + 1, rows, width), f32),
            pltpu.VMEM((2, tables * rows, GROUP * width), bf16),
            pltpu.VMEM((width, tables * rows), bf16),
            pltpu.VMEM((2 * rows, tables * rows), bf16),
            pltpu.VMEM((count, rows, width), bf16),
            pltpu.VMEM((count, rows, width), f32),
            pltpu.VMEM((count, rows, width), bf16),
            pltpu.VMEM((planes, cols, rows, width), bf16),
            pltpu.VMEM((planes, cols, rows, width), bf16),
            pltpu.VMEM((planes, aux_rows, width), bf16),
            pltpu.VMEM((cols, aux_rows, width), bf16),
            pltpu.VMEM((cols, planes * width, width), f32),
            pltpu.VMEM((cols, planes * width, width), bf16),
            pltpu.VMEM((cols, planes * width, width), bf16),
            pltpu.VMEM((rows, width), f32),
            pltpu.VMEM((cols, rows, width), bf16),
            pltpu.VMEM((cols, rows, width), bf16),
            pltpu.VMEM((cols, planes, rows, width), bf16),
            dma((CHUNKS,)),
            dma((2,)),
            dma((planes,)),
            dma((planes,)),
            dma((cols,)),
            dma((cols,)),
            dma((planes,)),
            dma((planes,)),
            dma((cols,)),
            dma((cols,)),
            dma((planes,)),
            dma((planes,)),
            dma((cols,)),
            dma((cols,)),
            dma((cols,)),
            dma((cols, planes)),
            dma((cols, planes)),
        ],
        compiler_params=pltpu.CompilerParams(
            collective_id=0, has_side_effects=True, vmem_limit_bytes=vmem_bytes
        ),
        name="cycle",
    )(last, amplitudes, factors, margin_table)

    whole = pltpu.VMEM((pairs, rows, width), bf16)
    return pl.pallas_call(
        update_kernel,
        out_shape=jax.ShapeDtypeStruct(amplitudes.shape, bf16),
        in_specs=[smem, smem, smem, vmem, vmem, vmem, anywhere, anywhere],
        out_specs=anywhere,
        scratch_shapes=[
            pltpu.VMEM((tables, count, rows, width), f32),
            pltpu.VMEM((width, pairs), f32),
            whole,
            whole,
            whole,
            dma((pairs // BLOCK,)),
            dma((pairs // BLOCK,)),
            dma((pairs // BLOCK,)),
        ],
        compiler_params=pltpu.CompilerParams(vmem_limit_bytes=vmem_bytes),
        name="update",
    )(
        margin_index, owner, occ_energy, cyc.reshape(count, rows, width), margin_table,
        vir_energy, amplitudes, k_term,
    )


def solution(mesh):
    placed = (
        P("pair", "aux", None),
        P("pair", "aux", None),
        P("pair", None, None),
        P("pair"),
        P("pair", "aux", None),
        P("pair", None),
        P(),
        P("pair", None),
    )
    return jax.shard_map(
        local, mesh=mesh, in_specs=placed, out_specs=P("pair", "aux", None), check_vma=False
    )
```
